256 devices in a mesh: seq: 32 (over x, z), head: 8 (over y, core).
Axes of the slice: x: 4, y: 4, z: 8, core: 2. Of those that a mesh axis runs over, the one named last changes fastest.
Arguments:
- latent_cache: bfloat16 [2048, 64, 576], P('seq'), may hold values from -6 to 6
- block_owner: int32 [2048], P('seq'), may hold values from 0 to 15, as said below
- block_index: int32 [2048], P('seq'), may hold values from 0 to 1016, as said below
- cache_lengths: int32 [16], replicated, may hold values from 1 to 65088, as said below
- query_nope: bfloat16 [2, 16, 128, 128], P(None, None, 'head'), may hold values from -6 to 6
- query_rope: bfloat16 [2, 16, 128, 64], P(None, None, 'head'), may hold values from -136 to 136
- new_latent: bfloat16 [2, 16, 576], replicated, may hold values from -6 to 6
- w_uk: bfloat16 [128, 128, 512], P('head'), may hold values from -0.25 to 0.25
- value_up_weight: bfloat16 [128, 512, 128], P('head'), may hold values from -0.25 to 0.25
- w_out: bfloat16 [16384, 7168], P('head', 'seq'), may hold values from -0.1875 to 0.1875
Outputs:
- attended: bfloat16 [16, 2, 7168], P('head', None, 'seq')
The draws below stay inside these ranges and needn't reach their ends.
Inputs may be any that keep to these rules, and one draw needn't show every extreme that they name: `block_owner`: every request owns at least one block; request r owns exactly ceil(cache_lengths[r] / 64) blocks, whose block_index values are 0 up to that count minus one. `block_index`: together with block_owner, names each block of each request exactly once; one request owns exactly (1017) blocks, no request more. `cache_lengths`: the blocks of all requests fill all 2048 slots.
All inputs are finite; a program needn't handle non-finite values.
Results may differ from the reference program's by a relative error of at most 0.015.
Values may be sent and summed in bfloat16 or wider, within the bound.
No kernel may reach another device: no remote copies, remote signals or barrier semaphores. Data moves between devices by JAX's collectives and lax.ppermute only.
A program may use at most 192 MiB of HBM per device.

```python
import jax
import jax.numpy as jnp
from jax import lax

H = 128
KVL = 512
ROPE = 64
NOPE = 128
VD = 128
D = 7168
BLK = 64
STEPS = 2
REQ = 16
SLOTS = 2048


def layout(key):
    leading_random_key, second_key, third_key, fourth_key = jax.random.split(key, 4)
    long_count = (SLOTS - REQ + 3) // 2
    rest = SLOTS - long_count
    later = jnp.sort(jax.random.permutation(leading_random_key, rest - 1)[:REQ - 2] + 1).astype(jnp.int32) + long_count
    cuts = jnp.concatenate([jnp.full((1,), long_count, jnp.int32), later])
    slot_ids = jnp.arange(SLOTS, dtype=jnp.int32)
    sorted_requests = jnp.sum(slot_ids[:, None] >= cuts[None, :], axis=1).astype(jnp.int32)
    starts = jnp.concatenate([jnp.zeros((1,), jnp.int32), cuts])
    ends = jnp.concatenate([cuts, jnp.full((1,), SLOTS, jnp.int32)])
    positions = slot_ids - starts[sorted_requests]
    order = jax.random.permutation(second_key, SLOTS)
    tails = jax.random.randint(third_key, (REQ,), 1, BLK + 1).astype(jnp.int32)
    tails = jnp.where(jnp.arange(REQ, dtype=jnp.int32) == 0, BLK, tails).astype(jnp.int32)
    ranked_lengths = ((ends - starts - 1) * BLK + tails).astype(jnp.int32)
    relabel = jax.random.permutation(fourth_key, REQ).astype(jnp.int32)
    owners = relabel[sorted_requests]
    lengths = ranked_lengths[jnp.argsort(relabel)]
    return (owners[order], positions[order], lengths)


def draw_block_owner(key, part):
    return layout(key)[0]


def draw_block_index(key, part):
    return layout(key)[1]


def draw_cache_lengths(key, part):
    return layout(key)[2]


def draw_query_rope(key, part):
    key = jax.random.fold_in(key, 7)
    random_root_key = jax.random.fold_in(key, 0)
    values = jnp.clip(jax.random.normal(random_root_key, (STEPS, REQ, H, ROPE), jnp.float32), -6.0, 6.0)
    return values.astype(jnp.bfloat16)


def block_scale(rng, dims, cuts, low, top_value):
    gain, own = 1.0, jax.random.fold_in(rng, 6)
    for axis_at, parts in cuts:
        draws = jnp.exp(jax.random.uniform(jax.random.fold_in(own, axis_at), (parts,), jnp.float32, low / len(cuts), top_value / len(cuts)))
        gain = gain * jnp.repeat(draws, dims[axis_at] // parts).reshape([-1 if axis == axis_at else 1 for axis in range(len(dims))])
    return gain


def normal_values(stream_key, shape, deviation, bound, shards=(), held_as=jnp.bfloat16):
    array = jax.random.normal(stream_key, shape, jnp.float32) * deviation
    if len(shards) > 0:
        array = block_scale(stream_key, shape, shards, -0.22, 0.18) * array
    return jnp.clip(array, min=-bound, max=bound).astype(held_as)


def setup_inputs(seed: int = 0) -> dict:
    splits = jax.random.split(jax.random.key(seed), 11)
    latent_cache = normal_values(splits[0], (SLOTS, BLK, KVL + ROPE), 1.0, 6.0, ((0, 32),))
    block_owner = draw_block_owner(jax.random.fold_in(splits[10], 71), 0)
    block_index = draw_block_index(jax.random.fold_in(splits[10], 71), 0)
    cache_lengths = draw_cache_lengths(jax.random.fold_in(splits[10], 71), 0)
    query_nope = normal_values(splits[4], (STEPS, REQ, H, NOPE), 1.0, 6.0, ((2, 8),))
    query_rope = draw_query_rope(jax.random.fold_in(splits[10], 71), 0)
    new_latent = normal_values(splits[6], (STEPS, REQ, KVL + ROPE), 1.0, 6.0)
    w_uk = normal_values(splits[7], (H, NOPE, KVL), KVL ** -0.5, 0.25, ((0, 8),))
    value_up_weight = normal_values(splits[8], (H, KVL, VD), KVL ** -0.5, 0.25, ((0, 8),))
    w_out = normal_values(splits[9], (H * VD, D), (H * VD // 16) ** -0.5, 0.1875, ((0, 8), (1, 32)))
    return {"latent_cache": latent_cache, "block_owner": block_owner, "block_index": block_index, "cache_lengths": cache_lengths, "query_nope": query_nope, "query_rope": query_rope, "new_latent": new_latent, "w_uk": w_uk, "value_up_weight": value_up_weight, "w_out": w_out}


NEG = -1.0e30


def finish(m, l, acc, q_items, keys, step_of):
    s = jnp.einsum('kc,kjc->kj', q_items.astype(jnp.float32), keys.astype(jnp.float32)) * ((NOPE + ROPE) ** -0.5)
    live = jnp.arange(STEPS)[None, :] <= step_of[:, None]
    s = jnp.where(live, s, NEG)
    top = jnp.maximum(m, jnp.max(s, axis=-1))
    factor = jnp.exp(m - top)
    weights = jnp.where(live, jnp.exp(s - top[:, None]), 0.0)
    total = l * factor + jnp.sum(weights, axis=-1)
    rounded = weights.astype(jnp.bfloat16).astype(jnp.float32)
    acc_t = acc * factor[:, None] + jnp.einsum('kj,kjc->kc', rounded, keys[..., :KVL].astype(jnp.float32))
    return (acc_t / total[:, None]).astype(jnp.bfloat16)


def reference(latent_cache, block_owner, block_index, cache_lengths, query_nope, query_rope, new_latent, w_uk, value_up_weight, w_out):
    q_lat = jnp.einsum('srhn,hnk->srhk', query_nope.astype(jnp.float32), w_uk.astype(jnp.float32)).astype(jnp.bfloat16)
    q_full = jnp.concatenate([q_lat, query_rope], axis=-1)
    scale = (NOPE + ROPE) ** -0.5

    def slot_scores(args):
        block, owner, index = args
        query = q_full[:, owner]
        s = jnp.einsum('shc,tc->sht', query.astype(jnp.float32), block.astype(jnp.float32)) * scale
        valid = index * BLK + jnp.arange(BLK, dtype=jnp.int32) < cache_lengths[owner]
        return jnp.where(valid[None, None, :], s, NEG)

    scores = lax.map(slot_scores, (latent_cache, block_owner, block_index))
    slot_max = jnp.max(scores, axis=-1)
    onehot = block_owner[None, :] == jnp.arange(REQ, dtype=jnp.int32)[:, None]
    req_max = jnp.max(jnp.where(onehot[:, :, None, None], slot_max[None], NEG), axis=1)
    slot_top = req_max[block_owner]

    def slot_acc(args):
        s, top, block = args
        weights = jnp.exp(s - top[..., None])
        rounded = weights.astype(jnp.bfloat16).astype(jnp.float32)
        return jnp.sum(weights, axis=-1), jnp.einsum('sht,tk->shk', rounded, block[:, :KVL].astype(jnp.float32))

    slot_l, slot_v = lax.map(slot_acc, (scores, slot_top, latent_cache))
    req_l = jax.ops.segment_sum(slot_l, block_owner, REQ)
    req_v = jax.ops.segment_sum(slot_v, block_owner, REQ)
    m = jnp.transpose(req_max, (1, 0, 2))
    l = jnp.transpose(req_l, (1, 0, 2))
    acc = jnp.transpose(req_v, (1, 0, 2, 3))
    items = STEPS * REQ * H
    keys = jnp.broadcast_to(jnp.transpose(new_latent, (1, 0, 2))[None, :, None], (STEPS, REQ, H, STEPS, KVL + ROPE))
    step_of = jnp.broadcast_to(jnp.arange(STEPS, dtype=jnp.int32)[:, None, None], (STEPS, REQ, H)).reshape(items)
    latent_output = finish(m.reshape(items), l.reshape(items), acc.reshape(items, KVL), q_full.reshape(items, KVL + ROPE), keys.reshape(items, STEPS, KVL + ROPE), step_of)
    latent_output = latent_output.reshape(STEPS, REQ, H, KVL)
    value_output = jnp.einsum('fiel,elx->fiex', latent_output.astype(jnp.float32), value_up_weight.astype(jnp.float32)).astype(jnp.bfloat16)
    rows = jnp.transpose(value_output, (1, 0, 2, 3)).reshape(REQ * STEPS, H * VD)
    out = jnp.dot(rows, w_out, preferred_element_type=jnp.float32)
    return out.reshape(REQ, STEPS, D).astype(jnp.bfloat16)
```

```python
import functools
import math

import jax
import jax.numpy as jnp
from jax import lax
from jax.experimental import pallas as pl
from jax.experimental.pallas import tpu as pltpu
from jax.sharding import PartitionSpec as P

KVL = 512
ROPE = 64
NOPE = 128
VD = 128
BLK = 64
LANES = 128
PITCH = 24

NEG = -1e30
SCALE = (NOPE + ROPE) ** (-0.5) * math.log2(math.e)
VMEM_LIMIT = 48 * 1024 * 1024
GROUP = 8

NT = (((1,), (1,)), ((), ()))


def attend(
    owner,
    index,
    lengths,
    query_nope,
    query_rope,
    new_latent,
    w_uk_hbm,
    value_up_hbm,
    cache_hbm,
    out,
    w_uk,
    value_up,
    cache,
    nope,
    q_lat,
    q_full,
    scores,
    best,
    top,
    part,
    acc,
    message,
    weight_sem,
    cache_sem,
):
    blocks = cache.shape[0]
    steps, requests, heads = query_nope.shape[:3]
    rows = steps * requests
    group = min(GROUP, blocks)
    chunks = blocks // group
    mine = lax.axis_index("seq")

    copy_uk = pltpu.make_async_copy(w_uk_hbm, w_uk, weight_sem.at[0])
    copy_up = pltpu.make_async_copy(value_up_hbm, value_up, weight_sem.at[1])

    def copy_chunk(i):
        span = pl.ds(i * group, group)
        return pltpu.make_async_copy(cache_hbm.at[span], cache.at[span], cache_sem.at[i])

    copy_uk.start()
    for i in range(chunks):
        copy_chunk(i).start()
    copy_up.start()

    nope[...] = query_nope[...].reshape(rows * heads, NOPE).astype(jnp.float32)
    best[...] = jnp.full(best.shape, NEG, jnp.float32)
    part[...] = jnp.zeros(part.shape, jnp.float32)
    acc[...] = jnp.zeros(acc.shape, jnp.float32)
    message[...] = jnp.zeros(message.shape, jnp.float32)

    copy_uk.wait()
    for h in range(heads):
        y = jnp.dot(
            nope[pl.ds(h, rows, stride=heads), :].astype(jnp.bfloat16),
            w_uk[h],
            preferred_element_type=jnp.float32,
        )
        for c in range(KVL // LANES):
            q_lat[c, pl.ds(h, rows, stride=heads), :] = y[:, c * LANES : (c + 1) * LANES]
    for r in range(requests):
        for s in range(steps):
            for c in range(KVL // LANES):
                q_full[r, s * heads : (s + 1) * heads, c * LANES : (c + 1) * LANES] = q_lat[
                    c, (s * requests + r) * heads : (s * requests + r + 1) * heads, :
                ].astype(jnp.bfloat16)
            q_full[r, s * heads : (s + 1) * heads, KVL:] = query_rope[s, r]

    lane = lax.broadcasted_iota(jnp.int32, (steps * heads, BLK), 1)

    def score_chunk(i, carry):
        copy_chunk(i).wait()
        for j in range(group):
            b = i * group + j
            o = owner[b]
            live = lengths[o] - index[b] * BLK
            s = lax.dot_general(q_full[o], cache[b], NT, preferred_element_type=jnp.float32)
            s = jnp.where(lane < live, s * SCALE, NEG)
            scores[b] = s
            best[o] = jnp.maximum(best[o], s)
        return carry

    lax.fori_loop(0, chunks, score_chunk, 0)

    taken = jnp.minimum(mine, requests - 1)
    shape = (steps * heads, steps * requests)
    token = lax.broadcasted_iota(jnp.int32, shape, 1)
    step = lax.broadcasted_iota(jnp.int32, shape, 0) // heads
    allowed = (token % requests == mine) & (token // requests <= step)
    keys = new_latent[...].reshape(steps * requests, KVL + ROPE)
    fresh = lax.dot_general(q_full[taken], keys, NT, preferred_element_type=jnp.float32)
    fresh = jnp.where(allowed, fresh * SCALE, NEG)
    best[taken, :, : steps * requests] = jnp.maximum(best[taken, :, : steps * requests], fresh)

    m = jnp.max(best[...], axis=-1, keepdims=True)
    high = m.astype(jnp.bfloat16).astype(jnp.float32)
    low = (m - high).astype(jnp.bfloat16).astype(jnp.float32)
    top[...] = jnp.broadcast_to(high + low, top.shape)

    def add(o, weights, values):
        y = jnp.dot(weights.astype(jnp.bfloat16), values, preferred_element_type=jnp.float32)
        span = pl.ds(pl.multiple_of(o * (steps * heads), steps * heads), steps * heads)
        for c in range(KVL // LANES):
            acc[c, span, :] += y[:, c * LANES : (c + 1) * LANES]

    def add_chunk(i, carry):
        for j in range(group):
            b = i * group + j
            o = owner[b]
            weights = jnp.exp2(scores[b] - top[o, :, :BLK])
            part[o] += weights
            add(o, weights, cache[b, :, :KVL])
        return carry

    lax.fori_loop(0, chunks, add_chunk, 0)
    weights = jnp.where(allowed, jnp.exp2(fresh - top[taken, :, : steps * requests]), 0.0)
    part[taken, :, : steps * requests] += weights
    add(taken, weights, keys[:, :KVL])

    total = jnp.sum(part[...], axis=-1, keepdims=True)
    best_rows = jnp.broadcast_to(total, top.shape).reshape(rows * heads, LANES)
    nope[...] = best_rows
    q_lat[0] = top[...].reshape(rows * heads, LANES)
    place = lax.broadcasted_iota(jnp.int32, (rows, LANES), 1)
    m_of = jnp.zeros((rows, LANES), jnp.float32)
    l_of = jnp.zeros((rows, LANES), jnp.float32)
    copy_up.wait()
    for h in range(heads):
        every = pl.ds(h, rows, stride=heads)
        x = jnp.concatenate([acc[c, every, :].astype(jnp.bfloat16) for c in range(KVL // LANES)], axis=-1)
        y = jnp.dot(x, value_up[h], preferred_element_type=jnp.float32)
        message[pl.ds(h, rows, stride=PITCH), :] = y
        m_of = jnp.where(place % heads == h, q_lat[0, every, :], m_of)
        l_of = jnp.where(place % heads == h, nope[every, :], l_of)
    m_high = m_of.astype(jnp.bfloat16).astype(jnp.float32)
    l_high = l_of.astype(jnp.bfloat16).astype(jnp.float32)
    kind = place // heads
    state = jnp.where(kind == 0, m_high, jnp.where(kind == 1, m_of - m_high, jnp.where(kind == 2, l_high, l_of - l_high)))
    message[pl.ds(heads, rows, stride=PITCH), :] = state
    out[...] = message[...].reshape(out.shape).astype(jnp.bfloat16)


def combine(parts, out, wide):
    count, pitch, _ = parts.shape
    heads = out.shape[1]
    wide[...] = parts[...].astype(jnp.float32).reshape(wide.shape)
    state = wide[pl.ds(heads, count, stride=pitch), :]
    joined = state + pltpu.roll(state, LANES - heads, 1)
    total = pltpu.roll(joined, LANES - 2 * heads, 1)
    place = lax.broadcasted_iota(jnp.int32, (count, LANES), 1)
    m = jnp.where(place < heads, joined, 0.0)
    l = jnp.where(place < heads, total, 1.0)
    factor = jnp.exp2(m - jnp.max(m, axis=0, keepdims=True))
    share = factor / jnp.sum(factor * l, axis=0, keepdims=True)
    turned = share.T[:heads, :]
    y = jnp.zeros((heads, LANES), jnp.float32)
    for k in range(count):
        y += turned[:, k : k + 1] * wide[pl.ds(k * pitch, heads), :]
    out[...] = jnp.broadcast_to(y.astype(jnp.bfloat16)[None], out.shape)


def project(values, w_out, out, wide):
    rows, heads, _ = values.shape
    wide[...] = values[...].astype(jnp.float32).reshape(wide.shape)
    x = jnp.concatenate(
        [wide[pl.ds(h, rows, stride=heads), :].astype(jnp.bfloat16) for h in range(heads)], axis=-1
    )
    y = jnp.dot(x, w_out[...], preferred_element_type=jnp.float32)
    each = out.shape[1]
    for j in range(out.shape[0]):
        out[j] = y[j * each : (j + 1) * each]


def local(
    head_devices,
    latent_cache,
    block_owner,
    block_index,
    cache_lengths,
    query_nope,
    query_rope,
    new_latent,
    w_uk,
    value_up_weight,
    w_out,
):
    steps, requests, heads = query_nope.shape[:3]
    rows = steps * requests
    blocks = latent_cache.shape[0]
    width = KVL + ROPE
    chunks = blocks // min(GROUP, blocks)
    vmem = pl.BlockSpec(memory_space=pltpu.VMEM)
    smem = pl.BlockSpec(memory_space=pltpu.SMEM)
    hbm = pl.BlockSpec(memory_space=pl.ANY)
    params = pltpu.CompilerParams(vmem_limit_bytes=VMEM_LIMIT)
    f32, bf16 = jnp.float32, jnp.bfloat16
    message = pl.pallas_call(
        attend,
        out_shape=jax.ShapeDtypeStruct((rows, PITCH, LANES), bf16),
        in_specs=[smem, smem, smem, vmem, vmem, vmem, hbm, hbm, hbm],
        out_specs=vmem,
        scratch_shapes=[
            pltpu.VMEM(w_uk.shape, bf16),
            pltpu.VMEM(value_up_weight.shape, bf16),
            pltpu.VMEM(latent_cache.shape, bf16),
            pltpu.VMEM((rows * heads, LANES), f32),
            pltpu.VMEM((KVL // LANES, rows * heads, LANES), f32),
            pltpu.VMEM((requests, steps * heads, width), bf16),
            pltpu.VMEM((blocks, steps * heads, BLK), f32),
            pltpu.VMEM((requests, steps * heads, BLK), f32),
            pltpu.VMEM((requests, steps * heads, LANES), f32),
            pltpu.VMEM((requests, steps * heads, BLK), f32),
            pltpu.VMEM((KVL // LANES, rows * heads, LANES), f32),
            pltpu.VMEM((rows * PITCH, LANES), f32),
            pltpu.SemaphoreType.DMA((2,)),
            pltpu.SemaphoreType.DMA((chunks,)),
        ],
        compiler_params=params,
        name="attend",
    )(
        block_owner,
        block_index,
        cache_lengths,
        query_nope,
        query_rope,
        new_latent,
        w_uk,
        value_up_weight,
        latent_cache,
    )
    parts = lax.all_to_all(message, "seq", 0, 0, tiled=True)
    value = pl.pallas_call(
        combine,
        out_shape=jax.ShapeDtypeStruct((rows, heads, VD), bf16),
        in_specs=[vmem],
        out_specs=vmem,
        scratch_shapes=[pltpu.VMEM((rows * PITCH, LANES), f32)],
        compiler_params=params,
        name="combine",
    )(parts)
    values = lax.all_to_all(value, "seq", 0, 0, tiled=True)
    sums = pl.pallas_call(
        project,
        out_shape=jax.ShapeDtypeStruct((head_devices, rows // head_devices, w_out.shape[1]), f32),
        in_specs=[vmem, vmem],
        out_specs=vmem,
        scratch_shapes=[pltpu.VMEM((rows * heads, LANES), f32)],
        compiler_params=params,
        name="project",
    )(values, w_out)
    sums = lax.all_to_all(sums, "head", 0, 0, tiled=True)
    return jnp.sum(sums, axis=0).reshape(requests // head_devices, steps, w_out.shape[1]).astype(bf16)


def solution(mesh):
    in_specs = (
        P("seq", None, None),
        P("seq"),
        P("seq"),
        P(),
        P(None, None, "head", None),
        P(None, None, "head", None),
        P(),
        P("head", None, None),
        P("head", None, None),
        P("head", "seq"),
    )
    out_specs = P("head", None, "seq")
    body = functools.partial(local, mesh.shape["head"])
    return jax.shard_map(body, mesh=mesh, in_specs=in_specs, out_specs=out_specs, check_vma=False)
```

```python
import functools
import math

import jax
import jax.numpy as jnp
from jax import lax
from jax.experimental import pallas as pl
from jax.experimental.pallas import tpu as pltpu
from jax.sharding import PartitionSpec as P

KVL = 512
ROPE = 64
NOPE = 128
VD = 128
BLK = 64
LANES = 128
PITCH = 24

NEG = -1e30
SCALE = (NOPE + ROPE) ** (-0.5) * math.log2(math.e)
VMEM_LIMIT = 60 * 1024 * 1024
GROUP = 32
KEY_PARTS = 4

NT = (((1,), (1,)), ((), ()))


def attend(
    owner_hbm,
    index_hbm,
    lengths_hbm,
    query_nope_hbm,
    query_rope_hbm,
    new_latent_hbm,
    w_uk_hbm,
    value_up_hbm,
    cache_hbm,
    out,
    owner,
    index,
    lengths,
    query_nope,
    query_rope,
    new_latent,
    w_uk,
    value_up,
    cache,
    nope,
    q_lat,
    q_full,
    scores,
    best,
    top,
    part,
    acc,
    message,
    small_sem,
    key_sem,
    value_sem,
    cache_sem,
):
    blocks = cache.shape[0]
    steps, requests, heads = query_nope_hbm.shape[:3]
    rows = steps * requests
    group = min(GROUP, blocks)
    chunks = blocks // group
    mine = lax.axis_index("seq")

    part_heads = heads // KEY_PARTS

    def copy_small(i, source, target):
        return pltpu.make_async_copy(source, target, small_sem.at[i])

    copy_nope = copy_small(0, query_nope_hbm, query_nope)
    others = [
        copy_small(i + 1, source, target)
        for i, (source, target) in enumerate(
            [
                (owner_hbm, owner),
                (index_hbm, index),
                (lengths_hbm, lengths),
                (query_rope_hbm, query_rope),
                (new_latent_hbm, new_latent),
            ]
        )
    ]

    def copy_uk(i):
        span = pl.ds(i * part_heads, part_heads)
        return pltpu.make_async_copy(w_uk_hbm.at[span], w_uk.at[span], key_sem.at[i])

    copy_up = pltpu.make_async_copy(value_up_hbm, value_up, value_sem)

    def copy_chunk(i):
        span = pl.ds(i * group, group)
        return pltpu.make_async_copy(cache_hbm.at[span], cache.at[span], cache_sem.at[i])

    copy_nope.start()
    for i in range(KEY_PARTS):
        copy_uk(i).start()
    for copy in others:
        copy.start()
    for i in range(chunks):
        copy_chunk(i).start()
    copy_up.start()

    best[...] = jnp.full(best.shape, NEG, jnp.float32)
    part[...] = jnp.zeros(part.shape, jnp.float32)
    acc[...] = jnp.zeros(acc.shape, jnp.float32)
    message[...] = jnp.zeros(message.shape, jnp.float32)

    copy_nope.wait()
    nope[...] = query_nope[...].reshape(rows * heads, NOPE).astype(jnp.float32)
    for h in range(heads):
        if h % part_heads == 0:
            copy_uk(h // part_heads).wait()
        y = jnp.dot(
            nope[pl.ds(h, rows, stride=heads), :].astype(jnp.bfloat16),
            w_uk[h],
            preferred_element_type=jnp.float32,
        )
        for c in range(KVL // LANES):
            q_lat[c, pl.ds(h, rows, stride=heads), :] = y[:, c * LANES : (c + 1) * LANES]
    for copy in others:
        copy.wait()
    for r in range(requests):
        for s in range(steps):
            for c in range(KVL // LANES):
                q_full[r, s * heads : (s + 1) * heads, c * LANES : (c + 1) * LANES] = q_lat[
                    c, (s * requests + r) * heads : (s * requests + r + 1) * heads, :
                ].astype(jnp.bfloat16)
            q_full[r, s * heads : (s + 1) * heads, KVL:] = query_rope[s, r]

    lane = lax.broadcasted_iota(jnp.int32, (steps * heads, BLK), 1)

    def score_chunk(i, carry):
        copy_chunk(i).wait()
        for j in range(group):
            b = i * group + j
            o = owner[b]
            live = lengths[o] - index[b] * BLK
            s = lax.dot_general(q_full[o], cache[b], NT, preferred_element_type=jnp.float32)
            s = jnp.where(lane < live, s * SCALE, NEG)
            scores[b] = s
            best[o] = jnp.maximum(best[o], s)
        return carry

    lax.fori_loop(0, chunks, score_chunk, 0)

    taken = jnp.minimum(mine, requests - 1)
    shape = (steps * heads, steps * requests)
    token = lax.broadcasted_iota(jnp.int32, shape, 1)
    step = lax.broadcasted_iota(jnp.int32, shape, 0) // heads
    allowed = (token % requests == mine) & (token // requests <= step)
    keys = new_latent[...].reshape(steps * requests, KVL + ROPE)
    fresh = lax.dot_general(q_full[taken], keys, NT, preferred_element_type=jnp.float32)
    fresh = jnp.where(allowed, fresh * SCALE, NEG)
    best[taken, :, : steps * requests] = jnp.maximum(best[taken, :, : steps * requests], fresh)

    m = jnp.max(best[...], axis=-1, keepdims=True)
    high = m.astype(jnp.bfloat16).astype(jnp.float32)
    low = (m - high).astype(jnp.bfloat16).astype(jnp.float32)
    top[...] = jnp.broadcast_to(high + low, top.shape)

    def add(o, weights, values):
        y = jnp.dot(weights.astype(jnp.bfloat16), values, preferred_element_type=jnp.float32)
        span = pl.ds(pl.multiple_of(o * (steps * heads), steps * heads), steps * heads)
        for c in range(KVL // LANES):
            acc[c, span, :] += y[:, c * LANES : (c + 1) * LANES]

    def add_chunk(i, carry):
        for j in range(min(64, blocks)):
            b = i * min(64, blocks) + j
            o = owner[b]
            weights = jnp.exp2(scores[b] - top[o, :, :BLK])
            part[o] += weights
            add(o, weights, cache[b, :, :KVL])
        return carry

    lax.fori_loop(0, blocks // min(64, blocks), add_chunk, 0)
    weights = jnp.where(allowed, jnp.exp2(fresh - top[taken, :, : steps * requests]), 0.0)
    part[taken, :, : steps * requests] += weights
    add(taken, weights, keys[:, :KVL])

    total = jnp.sum(part[...], axis=-1, keepdims=True)
    best_rows = jnp.broadcast_to(total, top.shape).reshape(rows * heads, LANES)
    nope[...] = best_rows
    q_lat[0] = top[...].reshape(rows * heads, LANES)
    place = lax.broadcasted_iota(jnp.int32, (rows, LANES), 1)
    m_of = jnp.zeros((rows, LANES), jnp.float32)
    l_of = jnp.zeros((rows, LANES), jnp.float32)
    copy_up.wait()
    for h in range(heads):
        every = pl.ds(h, rows, stride=heads)
        x = jnp.concatenate([acc[c, every, :].astype(jnp.bfloat16) for c in range(KVL // LANES)], axis=-1)
        y = jnp.dot(x, value_up[h], preferred_element_type=jnp.float32)
        message[pl.ds(h, rows, stride=PITCH), :] = y
        m_of = jnp.where(place % heads == h, q_lat[0, every, :], m_of)
        l_of = jnp.where(place % heads == h, nope[every, :], l_of)
    m_high = m_of.astype(jnp.bfloat16).astype(jnp.float32)
    l_high = l_of.astype(jnp.bfloat16).astype(jnp.float32)
    kind = place // heads
    state = jnp.where(kind == 0, m_high, jnp.where(kind == 1, m_of - m_high, jnp.where(kind == 2, l_high, l_of - l_high)))
    message[pl.ds(heads, rows, stride=PITCH), :] = state
    out[...] = message[...].reshape(out.shape).astype(jnp.bfloat16)


def combine(parts, out, wide):
    count, pitch, _ = parts.shape
    heads = out.shape[1]
    wide[...] = parts[...].astype(jnp.float32).reshape(wide.shape)
    state = wide[pl.ds(heads, count, stride=pitch), :]
    joined = state + pltpu.roll(state, LANES - heads, 1)
    total = pltpu.roll(joined, LANES - 2 * heads, 1)
    place = lax.broadcasted_iota(jnp.int32, (count, LANES), 1)
    m = jnp.where(place < heads, joined, 0.0)
    l = jnp.where(place < heads, total, 1.0)
    factor = jnp.exp2(m - jnp.max(m, axis=0, keepdims=True))
    share = factor / jnp.sum(factor * l, axis=0, keepdims=True)
    turned = share.T[:heads, :]
    y = jnp.zeros((heads, LANES), jnp.float32)
    for k in range(count):
        y += turned[:, k : k + 1] * wide[pl.ds(k * pitch, heads), :]
    out[...] = jnp.broadcast_to(y.astype(jnp.bfloat16)[None], out.shape)


def project(values, w_out, out, wide):
    rows, heads, _ = values.shape
    wide[...] = values[...].astype(jnp.float32).reshape(wide.shape)
    x = jnp.concatenate(
        [wide[pl.ds(h, rows, stride=heads), :].astype(jnp.bfloat16) for h in range(heads)], axis=-1
    )
    y = lax.dot_general(x, w_out[...], NT, preferred_element_type=jnp.float32)
    each = out.shape[1]
    for j in range(out.shape[0]):
        out[j] = y[j * each : (j + 1) * each]


def finish(sums, out):
    y = jnp.sum(sums[...], axis=0).astype(out.dtype)
    for r in range(out.shape[0]):
        out[r] = y[r * out.shape[1] : (r + 1) * out.shape[1]]


def local(
    head_devices,
    latent_cache,
    block_owner,
    block_index,
    cache_lengths,
    query_nope,
    query_rope,
    new_latent,
    w_uk,
    value_up_weight,
    w_out,
):
    steps, requests, heads = query_nope.shape[:3]
    rows = steps * requests
    blocks = latent_cache.shape[0]
    width = KVL + ROPE
    chunks = blocks // min(GROUP, blocks)
    vmem = pl.BlockSpec(memory_space=pltpu.VMEM)
    hbm = pl.BlockSpec(memory_space=pltpu.HBM)
    params = pltpu.CompilerParams(vmem_limit_bytes=VMEM_LIMIT)
    f32, bf16 = jnp.float32, jnp.bfloat16
    message = pl.pallas_call(
        attend,
        out_shape=jax.ShapeDtypeStruct((rows, PITCH, LANES), bf16),
        in_specs=[hbm] * 9,
        out_specs=vmem,
        scratch_shapes=[
            pltpu.SMEM(block_owner.shape, jnp.int32),
            pltpu.SMEM(block_index.shape, jnp.int32),
            pltpu.SMEM(cache_lengths.shape, jnp.int32),
            pltpu.VMEM(query_nope.shape, bf16),
            pltpu.VMEM(query_rope.shape, bf16),
            pltpu.VMEM(new_latent.shape, bf16),
            pltpu.VMEM(w_uk.shape, bf16),
            pltpu.VMEM(value_up_weight.shape, bf16),
            pltpu.VMEM(latent_cache.shape, bf16),
            pltpu.VMEM((rows * heads, LANES), f32),
            pltpu.VMEM((KVL // LANES, rows * heads, LANES), f32),
            pltpu.VMEM((requests, steps * heads, width), bf16),
            pltpu.VMEM((blocks, steps * heads, BLK), f32),
            pltpu.VMEM((requests, steps * heads, BLK), f32),
            pltpu.VMEM((requests, steps * heads, LANES), f32),
            pltpu.VMEM((requests, steps * heads, BLK), f32),
            pltpu.VMEM((KVL // LANES, rows * heads, LANES), f32),
            pltpu.VMEM((rows * PITCH, LANES), f32),
            pltpu.SemaphoreType.DMA((6,)),
            pltpu.SemaphoreType.DMA((KEY_PARTS,)),
            pltpu.SemaphoreType.DMA,
            pltpu.SemaphoreType.DMA((chunks,)),
        ],
        compiler_params=params,
        name="attend",
    )(
        block_owner,
        block_index,
        cache_lengths,
        query_nope,
        query_rope,
        new_latent,
        w_uk,
        value_up_weight,
        latent_cache,
    )
    parts = lax.all_to_all(message, "seq", 0, 0, tiled=True)
    value = pl.pallas_call(
        combine,
        out_shape=jax.ShapeDtypeStruct((rows, heads, VD), bf16),
        in_specs=[vmem],
        out_specs=vmem,
        scratch_shapes=[pltpu.VMEM((rows * PITCH, LANES), f32)],
        name="combine",
    )(parts)
    values = lax.all_to_all(value, "seq", 0, 0, tiled=True)
    sums = pl.pallas_call(
        project,
        out_shape=jax.ShapeDtypeStruct((head_devices, rows // head_devices, w_out.shape[1]), f32),
        in_specs=[vmem, vmem],
        out_specs=vmem,
        scratch_shapes=[pltpu.VMEM((rows * heads, LANES), f32)],
        name="project",
    )(values, w_out.T)
    sums = lax.all_to_all(sums, "head", 0, 0, tiled=True)
    return pl.pallas_call(
        finish,
        out_shape=jax.ShapeDtypeStruct((requests // head_devices, steps, w_out.shape[1]), bf16),
        in_specs=[vmem],
        out_specs=vmem,
        name="finish",
    )(sums)


def solution(mesh):
    in_specs = (
        P("seq", None, None),
        P("seq"),
        P("seq"),
        P(),
        P(None, None, "head", None),
        P(None, None, "head", None),
        P(),
        P("head", None, None),
        P("head", None, None),
        P("head", "seq"),
    )
    out_specs = P("head", None, "seq")
    body = functools.partial(local, mesh.shape["head"])
    return jax.shard_map(body, mesh=mesh, in_specs=in_specs, out_specs=out_specs, check_vma=False)
```

```python
import functools
import math

import jax
import jax.numpy as jnp
from jax import lax
from jax.experimental import pallas as pl
from jax.experimental.pallas import tpu as pltpu
from jax.sharding import PartitionSpec as P

KVL = 512
ROPE = 64
NOPE = 128
VD = 128
BLK = 64
LANES = 128
PITCH = 24

NEG = -1e30
SCALE = (NOPE + ROPE) ** (-0.5) * math.log2(math.e)
VMEM_LIMIT = 48 * 1024 * 1024
SMALL_LIMIT = 16 * 1024 * 1024
GROUP = 32
KEY_PARTS = 4

NT = (((1,), (1,)), ((), ()))


def attend(
    owner_hbm,
    index_hbm,
    lengths_hbm,
    query_nope_hbm,
    query_rope_hbm,
    new_latent_hbm,
    w_uk_hbm,
    value_up_hbm,
    cache_hbm,
    out,
    owner,
    index,
    lengths,
    query_nope,
    query_rope,
    new_latent,
    w_uk,
    value_up,
    cache,
    nope,
    q_lat,
    q_full,
    scores,
    best,
    top,
    part,
    acc,
    message,
    small_sem,
    key_sem,
    value_sem,
    cache_sem,
):
    blocks = cache.shape[0]
    steps, requests, heads = query_nope_hbm.shape[:3]
    rows = steps * requests
    group = min(GROUP, blocks)
    chunks = blocks // group
    mine = lax.axis_index("seq")

    part_heads = heads // KEY_PARTS

    def copy_small(i, source, target):
        return pltpu.make_async_copy(source, target, small_sem.at[i])

    copy_nope = copy_small(0, query_nope_hbm, query_nope)
    others = [
        copy_small(i + 1, source, target)
        for i, (source, target) in enumerate(
            [
                (owner_hbm, owner),
                (index_hbm, index),
                (lengths_hbm, lengths),
                (query_rope_hbm, query_rope),
                (new_latent_hbm, new_latent),
            ]
        )
    ]

    def copy_uk(i):
        span = pl.ds(i * part_heads, part_heads)
        return pltpu.make_async_copy(w_uk_hbm.at[span], w_uk.at[span], key_sem.at[i])

    copy_up = pltpu.make_async_copy(value_up_hbm, value_up, value_sem)

    def copy_chunk(i):
        span = pl.ds(i * group, group)
        return pltpu.make_async_copy(cache_hbm.at[span], cache.at[span], cache_sem.at[i])

    copy_nope.start()
    for i in range(KEY_PARTS):
        copy_uk(i).start()
    for copy in others:
        copy.start()
    for i in range(chunks):
        copy_chunk(i).start()
    copy_up.start()

    best[...] = jnp.full(best.shape, NEG, jnp.float32)
    part[...] = jnp.zeros(part.shape, jnp.float32)
    acc[...] = jnp.zeros(acc.shape, jnp.float32)
    message[...] = jnp.zeros(message.shape, jnp.float32)

    copy_nope.wait()
    nope[...] = query_nope[...].reshape(rows * heads, NOPE).astype(jnp.float32)
    for h in range(heads):
        if h % part_heads == 0:
            copy_uk(h // part_heads).wait()
        y = jnp.dot(
            nope[pl.ds(h, rows, stride=heads), :].astype(jnp.bfloat16),
            w_uk[h],
            preferred_element_type=jnp.float32,
        )
        for c in range(KVL // LANES):
            q_lat[c, pl.ds(h, rows, stride=heads), :] = y[:, c * LANES : (c + 1) * LANES]
    for copy in others:
        copy.wait()
    for r in range(requests):
        for s in range(steps):
            for c in range(KVL // LANES):
                q_full[r, s * heads : (s + 1) * heads, c * LANES : (c + 1) * LANES] = q_lat[
                    c, (s * requests + r) * heads : (s * requests + r + 1) * heads, :
                ].astype(jnp.bfloat16)
            q_full[r, s * heads : (s + 1) * heads, KVL:] = query_rope[s, r]

    lane = lax.broadcasted_iota(jnp.int32, (steps * heads, BLK), 1)

    def score_chunk(i, carry):
        copy_chunk(i).wait()
        for j in range(group):
            b = i * group + j
            o = owner[b]
            live = lengths[o] - index[b] * BLK
            s = lax.dot_general(q_full[o], cache[b], NT, preferred_element_type=jnp.float32)
            s = jnp.where(lane < live, s * SCALE, NEG)
            scores[b] = s
            best[o] = jnp.maximum(best[o], s)
        return carry

    for i in range(chunks):
        score_chunk(i, 0)

    taken = jnp.minimum(mine, requests - 1)
    shape = (steps * heads, steps * requests)
    token = lax.broadcasted_iota(jnp.int32, shape, 1)
    step = lax.broadcasted_iota(jnp.int32, shape, 0) // heads
    allowed = (token % requests == mine) & (token // requests <= step)
    keys = new_latent[...].reshape(steps * requests, KVL + ROPE)
    fresh = lax.dot_general(q_full[taken], keys, NT, preferred_element_type=jnp.float32)
    fresh = jnp.where(allowed, fresh * SCALE, NEG)
    best[taken, :, : steps * requests] = jnp.maximum(best[taken, :, : steps * requests], fresh)

    m = jnp.max(best[...], axis=-1, keepdims=True)
    high = m.astype(jnp.bfloat16).astype(jnp.float32)
    low = (m - high).astype(jnp.bfloat16).astype(jnp.float32)
    top[...] = jnp.broadcast_to(high + low, top.shape)

    def add(o, weights, values):
        y = jnp.dot(weights.astype(jnp.bfloat16), values, preferred_element_type=jnp.float32)
        span = pl.ds(pl.multiple_of(o * (steps * heads), steps * heads), steps * heads)
        for c in range(KVL // LANES):
            acc[c, span, :] += y[:, c * LANES : (c + 1) * LANES]

    def add_chunk(i, carry):
        for j in range(min(64, blocks)):
            b = i * min(64, blocks) + j
            o = owner[b]
            weights = jnp.exp2(scores[b] - top[o, :, :BLK])
            part[o] += weights
            add(o, weights, cache[b, :, :KVL])
        return carry

    lax.fori_loop(0, blocks // min(64, blocks), add_chunk, 0)
    weights = jnp.where(allowed, jnp.exp2(fresh - top[taken, :, : steps * requests]), 0.0)
    part[taken, :, : steps * requests] += weights
    add(taken, weights, keys[:, :KVL])

    total = jnp.sum(part[...], axis=-1, keepdims=True)
    best_rows = jnp.broadcast_to(total, top.shape).reshape(rows * heads, LANES)
    nope[...] = best_rows
    q_lat[0] = top[...].reshape(rows * heads, LANES)
    place = lax.broadcasted_iota(jnp.int32, (rows, LANES), 1)
    m_of = jnp.zeros((rows, LANES), jnp.float32)
    l_of = jnp.zeros((rows, LANES), jnp.float32)
    copy_up.wait()
    for h in range(heads):
        every = pl.ds(h, rows, stride=heads)
        x = jnp.concatenate([acc[c, every, :].astype(jnp.bfloat16) for c in range(KVL // LANES)], axis=-1)
        y = jnp.dot(x, value_up[h], preferred_element_type=jnp.float32)
        message[pl.ds(h, rows, stride=PITCH), :] = y
        m_of = jnp.where(place % heads == h, q_lat[0, every, :], m_of)
        l_of = jnp.where(place % heads == h, nope[every, :], l_of)
    m_high = m_of.astype(jnp.bfloat16).astype(jnp.float32)
    l_high = l_of.astype(jnp.bfloat16).astype(jnp.float32)
    kind = place // heads
    state = jnp.where(kind == 0, m_high, jnp.where(kind == 1, m_of - m_high, jnp.where(kind == 2, l_high, l_of - l_high)))
    message[pl.ds(heads, rows, stride=PITCH), :] = state
    out[...] = message[...].reshape(out.shape).astype(jnp.bfloat16)


def combine(parts, out, wide):
    count, pitch, _ = parts.shape
    heads = out.shape[1]
    wide[...] = parts[...].astype(jnp.float32).reshape(wide.shape)
    state = wide[pl.ds(heads, count, stride=pitch), :]
    joined = state + pltpu.roll(state, LANES - heads, 1)
    total = pltpu.roll(joined, LANES - 2 * heads, 1)
    place = lax.broadcasted_iota(jnp.int32, (count, LANES), 1)
    m = jnp.where(place < heads, joined, 0.0)
    l = jnp.where(place < heads, total, 1.0)
    factor = jnp.exp2(m - jnp.max(m, axis=0, keepdims=True))
    share = factor / jnp.sum(factor * l, axis=0, keepdims=True)
    turned = share.T[:heads, :]
    y = jnp.zeros((heads, LANES), jnp.float32)
    for k in range(count):
        y += turned[:, k : k + 1] * wide[pl.ds(k * pitch, heads), :]
    out[...] = jnp.broadcast_to(y.astype(jnp.bfloat16)[None], out.shape)


def project(values, w_out, out, wide):
    rows, heads, _ = values.shape
    wide[...] = values[...].astype(jnp.float32).reshape(wide.shape)
    x = jnp.concatenate(
        [wide[pl.ds(h, rows, stride=heads), :].astype(jnp.bfloat16) for h in range(heads)], axis=-1
    )
    y = lax.dot_general(x, w_out[...], NT, preferred_element_type=jnp.float32)
    each = out.shape[1]
    for j in range(out.shape[0]):
        out[j] = y[j * each : (j + 1) * each]


def finish(sums, out):
    y = jnp.sum(sums[...], axis=0).astype(out.dtype)
    for r in range(out.shape[0]):
        out[r] = y[r * out.shape[1] : (r + 1) * out.shape[1]]


def local(
    head_devices,
    latent_cache,
    block_owner,
    block_index,
    cache_lengths,
    query_nope,
    query_rope,
    new_latent,
    w_uk,
    value_up_weight,
    w_out,
):
    steps, requests, heads = query_nope.shape[:3]
    rows = steps * requests
    blocks = latent_cache.shape[0]
    width = KVL + ROPE
    chunks = blocks // min(GROUP, blocks)
    vmem = pl.BlockSpec(memory_space=pltpu.VMEM)
    hbm = pl.BlockSpec(memory_space=pltpu.HBM)
    params = pltpu.CompilerParams(vmem_limit_bytes=VMEM_LIMIT)
    f32, bf16 = jnp.float32, jnp.bfloat16
    message = pl.pallas_call(
        attend,
        out_shape=pltpu.VMEM((rows, PITCH, LANES), bf16),
        in_specs=[hbm] * 9,
        out_specs=vmem,
        scratch_shapes=[
            pltpu.SMEM(block_owner.shape, jnp.int32),
            pltpu.SMEM(block_index.shape, jnp.int32),
            pltpu.SMEM(cache_lengths.shape, jnp.int32),
            pltpu.VMEM(query_nope.shape, bf16),
            pltpu.VMEM(query_rope.shape, bf16),
            pltpu.VMEM(new_latent.shape, bf16),
            pltpu.VMEM(w_uk.shape, bf16),
            pltpu.VMEM(value_up_weight.shape, bf16),
            pltpu.VMEM(latent_cache.shape, bf16),
            pltpu.VMEM((rows * heads, LANES), f32),
            pltpu.VMEM((KVL // LANES, rows * heads, LANES), f32),
            pltpu.VMEM((requests, steps * heads, width), bf16),
            pltpu.VMEM((blocks, steps * heads, BLK), f32),
            pltpu.VMEM((requests, steps * heads, BLK), f32),
            pltpu.VMEM((requests, steps * heads, LANES), f32),
            pltpu.VMEM((requests, steps * heads, BLK), f32),
            pltpu.VMEM((KVL // LANES, rows * heads, LANES), f32),
            pltpu.VMEM((rows * PITCH, LANES), f32),
            pltpu.SemaphoreType.DMA((6,)),
            pltpu.SemaphoreType.DMA((KEY_PARTS,)),
            pltpu.SemaphoreType.DMA,
            pltpu.SemaphoreType.DMA((chunks,)),
        ],
        compiler_params=params,
        name="attend",
    )(
        *(
            pltpu.with_memory_space_constraint(x, pltpu.HBM)
            for x in (
                block_owner,
                block_index,
                cache_lengths,
                query_nope,
                query_rope,
                new_latent,
                w_uk,
                value_up_weight,
                latent_cache,
            )
        )
    )
    parts = lax.all_to_all(message, "seq", 0, 0, tiled=True)
    value = pl.pallas_call(
        combine,
        out_shape=jax.ShapeDtypeStruct((rows, heads, VD), bf16),
        in_specs=[vmem],
        out_specs=vmem,
        scratch_shapes=[pltpu.VMEM((rows * PITCH, LANES), f32)],
        compiler_params=pltpu.CompilerParams(vmem_limit_bytes=SMALL_LIMIT),
        name="combine",
    )(parts)
    values = lax.all_to_all(value, "seq", 0, 0, tiled=True)
    sums = pl.pallas_call(
        project,
        out_shape=jax.ShapeDtypeStruct((head_devices, rows // head_devices, w_out.shape[1]), f32),
        in_specs=[vmem, vmem],
        out_specs=vmem,
        scratch_shapes=[pltpu.VMEM((rows * heads, LANES), f32)],
        compiler_params=pltpu.CompilerParams(vmem_limit_bytes=SMALL_LIMIT),
        name="project",
    )(values, w_out.T)
    sums = lax.all_to_all(sums, "head", 0, 0, tiled=True)
    return pl.pallas_call(
        finish,
        out_shape=jax.ShapeDtypeStruct((requests // head_devices, steps, w_out.shape[1]), bf16),
        in_specs=[vmem],
        out_specs=vmem,
        compiler_params=pltpu.CompilerParams(vmem_limit_bytes=SMALL_LIMIT),
        name="finish",
    )(sums)


def solution(mesh):
    in_specs = (
        P("seq", None, None),
        P("seq"),
        P("seq"),
        P(),
        P(None, None, "head", None),
        P(None, None, "head", None),
        P(),
        P("head", None, None),
        P("head", None, None),
        P("head", "seq"),
    )
    out_specs = P("head", None, "seq")
    body = functools.partial(local, mesh.shape["head"])
    return jax.shard_map(body, mesh=mesh, in_specs=in_specs, out_specs=out_specs, check_vma=False)
```

```python
import functools
import math

import jax
import jax.numpy as jnp
from jax import lax
from jax.experimental import pallas as pl
from jax.experimental.pallas import tpu as pltpu
from jax.sharding import PartitionSpec as P

KVL = 512
ROPE = 64
NOPE = 128
VD = 128
BLK = 64
LANES = 128
PITCH = 18
THIN = 2

NEG = -1e30
SCALE = (NOPE + ROPE) ** (-0.5) * math.log2(math.e)
VMEM_LIMIT = 48 * 1024 * 1024
SMALL_LIMIT = 16 * 1024 * 1024
GROUP = 32
KEY_PARTS = 4

NT = (((1,), (1,)), ((), ()))


def attend(
    owner_hbm,
    index_hbm,
    lengths_hbm,
    query_nope_hbm,
    query_rope_hbm,
    new_latent_hbm,
    w_uk_hbm,
    value_up_hbm,
    cache_hbm,
    out,
    owner,
    index,
    lengths,
    query_nope,
    query_rope,
    new_latent,
    w_uk,
    value_up,
    cache,
    nope,
    q_lat,
    q_full,
    scores,
    best,
    top,
    part,
    acc,
    message,
    small_sem,
    key_sem,
    value_sem,
    cache_sem,
):
    blocks = cache.shape[0]
    steps, requests, heads = query_nope_hbm.shape[:3]
    rows = steps * requests
    group = min(GROUP, blocks)
    chunks = blocks // group
    mine = lax.axis_index("seq")

    part_heads = heads // KEY_PARTS

    def copy_small(i, source, target):
        return pltpu.make_async_copy(source, target, small_sem.at[i])

    copy_nope = copy_small(0, query_nope_hbm, query_nope)
    others = [
        copy_small(i + 1, source, target)
        for i, (source, target) in enumerate(
            [
                (owner_hbm, owner),
                (index_hbm, index),
                (lengths_hbm, lengths),
                (query_rope_hbm, query_rope),
                (new_latent_hbm, new_latent),
            ]
        )
    ]

    def copy_uk(i):
        span = pl.ds(i * part_heads, part_heads)
        return pltpu.make_async_copy(w_uk_hbm.at[span], w_uk.at[span], key_sem.at[i])

    copy_up = pltpu.make_async_copy(value_up_hbm, value_up, value_sem)

    def copy_chunk(i):
        span = pl.ds(i * group, group)
        return pltpu.make_async_copy(cache_hbm.at[span], cache.at[span], cache_sem.at[i])

    copy_nope.start()
    for i in range(KEY_PARTS):
        copy_uk(i).start()
    for copy in others:
        copy.start()
    for i in range(chunks):
        copy_chunk(i).start()
    copy_up.start()

    best[...] = jnp.full(best.shape, NEG, jnp.float32)
    part[...] = jnp.zeros(part.shape, jnp.float32)
    acc[...] = jnp.zeros(acc.shape, jnp.float32)
    message[...] = jnp.zeros(message.shape, jnp.float32)

    copy_nope.wait()
    nope[...] = query_nope[...].reshape(rows * heads, NOPE).astype(jnp.float32)
    for h in range(heads):
        if h % part_heads == 0:
            copy_uk(h // part_heads).wait()
        y = jnp.dot(
            nope[pl.ds(h, rows, stride=heads), :].astype(jnp.bfloat16),
            w_uk[h],
            preferred_element_type=jnp.float32,
        )
        for c in range(KVL // LANES):
            q_lat[c, pl.ds(h, rows, stride=heads), :] = y[:, c * LANES : (c + 1) * LANES]
    for copy in others:
        copy.wait()
    for r in range(requests):
        for s in range(steps):
            for c in range(KVL // LANES):
                q_full[r, s * heads : (s + 1) * heads, c * LANES : (c + 1) * LANES] = q_lat[
                    c, (s * requests + r) * heads : (s * requests + r + 1) * heads, :
                ].astype(jnp.bfloat16)
            q_full[r, s * heads : (s + 1) * heads, KVL:] = query_rope[s, r]

    lane = lax.broadcasted_iota(jnp.int32, (steps * heads, BLK), 1)

    def score_chunk(i, carry):
        copy_chunk(i).wait()
        for j in range(group):
            b = i * group + j
            o = owner[b]
            live = lengths[o] - index[b] * BLK
            s = lax.dot_general(q_full[o], cache[b], NT, preferred_element_type=jnp.float32)
            s = jnp.where(lane < live, s * SCALE, NEG)
            scores[b] = s
            best[o] = jnp.maximum(best[o], s)
        return carry

    for i in range(chunks):
        score_chunk(i, 0)

    taken = jnp.minimum(mine, requests - 1)
    shape = (steps * heads, steps * requests)
    token = lax.broadcasted_iota(jnp.int32, shape, 1)
    step = lax.broadcasted_iota(jnp.int32, shape, 0) // heads
    allowed = (token % requests == mine) & (token // requests <= step)
    keys = new_latent[...].reshape(steps * requests, KVL + ROPE)
    fresh = lax.dot_general(q_full[taken], keys, NT, preferred_element_type=jnp.float32)
    fresh = jnp.where(allowed, fresh * SCALE, NEG)
    best[taken, :, : steps * requests] = jnp.maximum(best[taken, :, : steps * requests], fresh)

    m = jnp.max(best[...], axis=-1, keepdims=True)
    high = m.astype(jnp.bfloat16).astype(jnp.float32)
    low = (m - high).astype(jnp.bfloat16).astype(jnp.float32)
    top[...] = jnp.broadcast_to(high + low, top.shape)

    def add(o, weights, values):
        y = jnp.dot(weights.astype(jnp.bfloat16), values, preferred_element_type=jnp.float32)
        span = pl.ds(pl.multiple_of(o * (steps * heads), steps * heads), steps * heads)
        for c in range(KVL // LANES):
            acc[c, span, :] += y[:, c * LANES : (c + 1) * LANES]

    def add_chunk(i, carry):
        for j in range(min(64, blocks)):
            b = i * min(64, blocks) + j
            o = owner[b]
            weights = jnp.exp2(scores[b] - top[o, :, :BLK])
            part[o] += weights
            add(o, weights, cache[b, :, :KVL])
        return carry

    lax.fori_loop(0, blocks // min(64, blocks), add_chunk, 0)
    weights = jnp.where(allowed, jnp.exp2(fresh - top[taken, :, : steps * requests]), 0.0)
    part[taken, :, : steps * requests] += weights
    add(taken, weights, keys[:, :KVL])

    total = jnp.sum(part[...], axis=-1, keepdims=True)
    best_rows = jnp.broadcast_to(total, top.shape).reshape(rows * heads, LANES)
    nope[...] = best_rows
    q_lat[0] = top[...].reshape(rows * heads, LANES)
    place = lax.broadcasted_iota(jnp.int32, (rows, LANES), 1)
    m_of = jnp.zeros((rows, LANES), jnp.float32)
    l_of = jnp.zeros((rows, LANES), jnp.float32)
    copy_up.wait()
    for h in range(heads):
        every = pl.ds(h, rows, stride=heads)
        x = jnp.concatenate([acc[c, every, :].astype(jnp.bfloat16) for c in range(KVL // LANES)], axis=-1)
        y = jnp.dot(x, value_up[h], preferred_element_type=jnp.float32)
        message[pl.ds(h, rows, stride=PITCH), :] = y
        m_of = jnp.where(place % heads == h, q_lat[0, every, :], m_of)
        l_of = jnp.where(place % heads == h, nope[every, :], l_of)
    m_high = m_of.astype(jnp.bfloat16).astype(jnp.float32)
    l_high = l_of.astype(jnp.bfloat16).astype(jnp.float32)
    kind = place // heads
    state = jnp.where(kind == 0, m_high, jnp.where(kind == 1, m_of - m_high, jnp.where(kind == 2, l_high, l_of - l_high)))
    message[pl.ds(heads, rows, stride=PITCH), :] = state
    out[...] = message[...].reshape(out.shape).astype(jnp.bfloat16)


def combine(parts, out, wide):
    count, pitch = parts.shape[0], PITCH
    heads = out.shape[1]
    wide[...] = parts[...].astype(jnp.float32).reshape(wide.shape)
    state = wide[pl.ds(heads, count, stride=pitch), :]
    joined = state + pltpu.roll(state, LANES - heads, 1)
    total = pltpu.roll(joined, LANES - 2 * heads, 1)
    place = lax.broadcasted_iota(jnp.int32, (count, LANES), 1)
    m = jnp.where(place < heads, joined, 0.0)
    l = jnp.where(place < heads, total, 1.0)
    factor = jnp.exp2(m - jnp.max(m, axis=0, keepdims=True))
    share = factor / jnp.sum(factor * l, axis=0, keepdims=True)
    turned = share.T[:heads, :]
    y = jnp.zeros((heads, LANES), jnp.float32)
    for k in range(count):
        y += turned[:, k : k + 1] * wide[pl.ds(k * pitch, heads), :]
    out[...] = jnp.broadcast_to(y.astype(jnp.bfloat16)[None], out.shape)


def project(values, w_out, out, wide):
    rows, heads, _ = values.shape
    wide[...] = values[...].astype(jnp.float32).reshape(wide.shape)
    x = jnp.concatenate(
        [wide[pl.ds(h, rows, stride=heads), :].astype(jnp.bfloat16) for h in range(heads)], axis=-1
    )
    y = lax.dot_general(x, w_out[...], NT, preferred_element_type=jnp.float32)
    each = out.shape[1]
    for j in range(out.shape[0]):
        out[j] = y[j * each : (j + 1) * each]


def finish(sums, out):
    y = jnp.sum(sums[...], axis=0).astype(out.dtype)
    for r in range(out.shape[0]):
        out[r] = y[r * out.shape[1] : (r + 1) * out.shape[1]]


def local(
    head_devices,
    latent_cache,
    block_owner,
    block_index,
    cache_lengths,
    query_nope,
    query_rope,
    new_latent,
    w_uk,
    value_up_weight,
    w_out,
):
    steps, requests, heads = query_nope.shape[:3]
    rows = steps * requests
    blocks = latent_cache.shape[0]
    width = KVL + ROPE
    chunks = blocks // min(GROUP, blocks)
    vmem = pl.BlockSpec(memory_space=pltpu.VMEM)
    hbm = pl.BlockSpec(memory_space=pltpu.HBM)
    params = pltpu.CompilerParams(vmem_limit_bytes=VMEM_LIMIT)
    f32, bf16 = jnp.float32, jnp.bfloat16
    message = pl.pallas_call(
        attend,
        out_shape=pltpu.VMEM((rows, PITCH // THIN, THIN, LANES), bf16),
        in_specs=[hbm] * 9,
        out_specs=vmem,
        scratch_shapes=[
            pltpu.SMEM(block_owner.shape, jnp.int32),
            pltpu.SMEM(block_index.shape, jnp.int32),
            pltpu.SMEM(cache_lengths.shape, jnp.int32),
            pltpu.VMEM(query_nope.shape, bf16),
            pltpu.VMEM(query_rope.shape, bf16),
            pltpu.VMEM(new_latent.shape, bf16),
            pltpu.VMEM(w_uk.shape, bf16),
            pltpu.VMEM(value_up_weight.shape, bf16),
            pltpu.VMEM(latent_cache.shape, bf16),
            pltpu.VMEM((rows * heads, LANES), f32),
            pltpu.VMEM((KVL // LANES, rows * heads, LANES), f32),
            pltpu.VMEM((requests, steps * heads, width), bf16),
            pltpu.VMEM((blocks, steps * heads, BLK), f32),
            pltpu.VMEM((requests, steps * heads, BLK), f32),
            pltpu.VMEM((requests, steps * heads, LANES), f32),
            pltpu.VMEM((requests, steps * heads, BLK), f32),
            pltpu.VMEM((KVL // LANES, rows * heads, LANES), f32),
            pltpu.VMEM((rows * PITCH, LANES), f32),
            pltpu.SemaphoreType.DMA((6,)),
            pltpu.SemaphoreType.DMA((KEY_PARTS,)),
            pltpu.SemaphoreType.DMA,
            pltpu.SemaphoreType.DMA((chunks,)),
        ],
        compiler_params=params,
        name="attend",
    )(
        *(
            pltpu.with_memory_space_constraint(x, pltpu.HBM)
            for x in (
                block_owner,
                block_index,
                cache_lengths,
                query_nope,
                query_rope,
                new_latent,
                w_uk,
                value_up_weight,
                latent_cache,
            )
        )
    )
    parts = lax.all_to_all(message, "seq", 0, 0, tiled=True)
    value = pl.pallas_call(
        combine,
        out_shape=jax.ShapeDtypeStruct((rows, heads, VD), bf16),
        in_specs=[vmem],
        out_specs=vmem,
        scratch_shapes=[pltpu.VMEM((rows * PITCH, LANES), f32)],
        compiler_params=pltpu.CompilerParams(vmem_limit_bytes=SMALL_LIMIT),
        name="combine",
    )(parts)
    values = lax.all_to_all(value, "seq", 0, 0, tiled=True)
    sums = pl.pallas_call(
        project,
        out_shape=jax.ShapeDtypeStruct((head_devices, rows // head_devices, w_out.shape[1]), f32),
        in_specs=[vmem, vmem],
        out_specs=vmem,
        scratch_shapes=[pltpu.VMEM((rows * heads, LANES), f32)],
        compiler_params=pltpu.CompilerParams(vmem_limit_bytes=SMALL_LIMIT),
        name="project",
    )(values, w_out.T)
    sums = lax.all_to_all(sums, "head", 0, 0, tiled=True)
    return pl.pallas_call(
        finish,
        out_shape=jax.ShapeDtypeStruct((requests // head_devices, steps, w_out.shape[1]), bf16),
        in_specs=[vmem],
        out_specs=vmem,
        compiler_params=pltpu.CompilerParams(vmem_limit_bytes=SMALL_LIMIT),
        name="finish",
    )(sums)


def solution(mesh):
    in_specs = (
        P("seq", None, None),
        P("seq"),
        P("seq"),
        P(),
        P(None, None, "head", None),
        P(None, None, "head", None),
        P(),
        P("head", None, None),
        P("head", None, None),
        P("head", "seq"),
    )
    out_specs = P("head", None, "seq")
    body = functools.partial(local, mesh.shape["head"])
    return jax.shard_map(body, mesh=mesh, in_specs=in_specs, out_specs=out_specs, check_vma=False)
```

```python
import functools
import math

import jax
import jax.numpy as jnp
from jax import lax
from jax.experimental import pallas as pl
from jax.experimental.pallas import tpu as pltpu
from jax.sharding import PartitionSpec as P

KVL = 512
ROPE = 64
NOPE = 128
VD = 128
BLK = 64
LANES = 128
PITCH = 18
THIN = 2

NEG = -1e30
SCALE = (NOPE + ROPE) ** (-0.5) * math.log2(math.e)
VMEM_LIMIT = 48 * 1024 * 1024
SMALL_LIMIT = 16 * 1024 * 1024
GROUP = 32
KEY_PARTS = 4

NT = (((1,), (1,)), ((), ()))


def attend(
    owner_hbm,
    index_hbm,
    lengths_hbm,
    query_nope_hbm,
    query_rope_hbm,
    new_latent_hbm,
    w_uk_hbm,
    value_up_hbm,
    cache_hbm,
    w_out_hbm,
    out,
    w_out,
    owner,
    index,
    lengths,
    query_nope,
    query_rope,
    new_latent,
    w_uk,
    value_up,
    cache,
    nope,
    q_lat,
    q_full,
    scores,
    best,
    top,
    part,
    acc,
    message,
    small_sem,
    key_sem,
    value_sem,
    out_sem,
    cache_sem,
):
    blocks = cache.shape[0]
    steps, requests, heads = query_nope_hbm.shape[:3]
    rows = steps * requests
    group = min(GROUP, blocks)
    chunks = blocks // group
    mine = lax.axis_index("seq")

    part_heads = heads // KEY_PARTS

    def copy_small(i, source, target):
        return pltpu.make_async_copy(source, target, small_sem.at[i])

    copy_nope = copy_small(0, query_nope_hbm, query_nope)
    others = [
        copy_small(i + 1, source, target)
        for i, (source, target) in enumerate(
            [
                (owner_hbm, owner),
                (index_hbm, index),
                (lengths_hbm, lengths),
                (query_rope_hbm, query_rope),
                (new_latent_hbm, new_latent),
            ]
        )
    ]

    def copy_uk(i):
        span = pl.ds(i * part_heads, part_heads)
        return pltpu.make_async_copy(w_uk_hbm.at[span], w_uk.at[span], key_sem.at[i])

    copy_up = pltpu.make_async_copy(value_up_hbm, value_up, value_sem)
    copy_out = pltpu.make_async_copy(w_out_hbm, w_out, out_sem)

    def copy_chunk(i):
        span = pl.ds(i * group, group)
        return pltpu.make_async_copy(cache_hbm.at[span], cache.at[span], cache_sem.at[i])

    copy_nope.start()
    for i in range(KEY_PARTS):
        copy_uk(i).start()
    for copy in others:
        copy.start()
    for i in range(chunks):
        copy_chunk(i).start()
    copy_up.start()
    copy_out.start()

    best[...] = jnp.full(best.shape, NEG, jnp.float32)
    part[...] = jnp.zeros(part.shape, jnp.float32)
    acc[...] = jnp.zeros(acc.shape, jnp.float32)
    message[...] = jnp.zeros(message.shape, jnp.float32)

    copy_nope.wait()
    nope[...] = query_nope[...].reshape(rows * heads, NOPE).astype(jnp.float32)
    for h in range(heads):
        if h % part_heads == 0:
            copy_uk(h // part_heads).wait()
        y = jnp.dot(
            nope[pl.ds(h, rows, stride=heads), :].astype(jnp.bfloat16),
            w_uk[h],
            preferred_element_type=jnp.float32,
        )
        for c in range(KVL // LANES):
            q_lat[c, pl.ds(h, rows, stride=heads), :] = y[:, c * LANES : (c + 1) * LANES]
    for copy in others:
        copy.wait()
    for r in range(requests):
        for s in range(steps):
            for c in range(KVL // LANES):
                q_full[r, s * heads : (s + 1) * heads, c * LANES : (c + 1) * LANES] = q_lat[
                    c, (s * requests + r) * heads : (s * requests + r + 1) * heads, :
                ].astype(jnp.bfloat16)
            q_full[r, s * heads : (s + 1) * heads, KVL:] = query_rope[s, r]

    lane = lax.broadcasted_iota(jnp.int32, (steps * heads, BLK), 1)

    def score_chunk(i, carry):
        copy_chunk(i).wait()
        for j in range(group):
            b = i * group + j
            o = owner[b]
            live = lengths[o] - index[b] * BLK
            s = lax.dot_general(q_full[o], cache[b], NT, preferred_element_type=jnp.float32)
            s = jnp.where(lane < live, s * SCALE, NEG)
            scores[b] = s
            best[o] = jnp.maximum(best[o], s)
        return carry

    for i in range(chunks):
        score_chunk(i, 0)

    taken = jnp.minimum(mine, requests - 1)
    shape = (steps * heads, steps * requests)
    token = lax.broadcasted_iota(jnp.int32, shape, 1)
    step = lax.broadcasted_iota(jnp.int32, shape, 0) // heads
    allowed = (token % requests == mine) & (token // requests <= step)
    keys = new_latent[...].reshape(steps * requests, KVL + ROPE)
    fresh = lax.dot_general(q_full[taken], keys, NT, preferred_element_type=jnp.float32)
    fresh = jnp.where(allowed, fresh * SCALE, NEG)
    best[taken, :, : steps * requests] = jnp.maximum(best[taken, :, : steps * requests], fresh)

    m = jnp.max(best[...], axis=-1, keepdims=True)
    high = m.astype(jnp.bfloat16).astype(jnp.float32)
    low = (m - high).astype(jnp.bfloat16).astype(jnp.float32)
    top[...] = jnp.broadcast_to(high + low, top.shape)

    def add(o, weights, values):
        y = jnp.dot(weights.astype(jnp.bfloat16), values, preferred_element_type=jnp.float32)
        span = pl.ds(pl.multiple_of(o * (steps * heads), steps * heads), steps * heads)
        for c in range(KVL // LANES):
            acc[c, span, :] += y[:, c * LANES : (c + 1) * LANES]

    def add_chunk(i, carry):
        for j in range(min(64, blocks)):
            b = i * min(64, blocks) + j
            o = owner[b]
            weights = jnp.exp2(scores[b] - top[o, :, :BLK])
            part[o] += weights
            add(o, weights, cache[b, :, :KVL])
        return carry

    lax.fori_loop(0, blocks // min(64, blocks), add_chunk, 0)
    weights = jnp.where(allowed, jnp.exp2(fresh - top[taken, :, : steps * requests]), 0.0)
    part[taken, :, : steps * requests] += weights
    add(taken, weights, keys[:, :KVL])

    total = jnp.sum(part[...], axis=-1, keepdims=True)
    best_rows = jnp.broadcast_to(total, top.shape).reshape(rows * heads, LANES)
    nope[...] = best_rows
    q_lat[0] = top[...].reshape(rows * heads, LANES)
    place = lax.broadcasted_iota(jnp.int32, (rows, LANES), 1)
    m_of = jnp.zeros((rows, LANES), jnp.float32)
    l_of = jnp.zeros((rows, LANES), jnp.float32)
    copy_up.wait()
    for h in range(heads):
        every = pl.ds(h, rows, stride=heads)
        x = jnp.concatenate([acc[c, every, :].astype(jnp.bfloat16) for c in range(KVL // LANES)], axis=-1)
        y = jnp.dot(x, value_up[h], preferred_element_type=jnp.float32)
        message[pl.ds(h, rows, stride=PITCH), :] = y
        m_of = jnp.where(place % heads == h, q_lat[0, every, :], m_of)
        l_of = jnp.where(place % heads == h, nope[every, :], l_of)
    m_high = m_of.astype(jnp.bfloat16).astype(jnp.float32)
    l_high = l_of.astype(jnp.bfloat16).astype(jnp.float32)
    kind = place // heads
    state = jnp.where(kind == 0, m_high, jnp.where(kind == 1, m_of - m_high, jnp.where(kind == 2, l_high, l_of - l_high)))
    message[pl.ds(heads, rows, stride=PITCH), :] = state
    out[...] = message[...].reshape(out.shape).astype(jnp.bfloat16)
    copy_out.wait()


def combine(parts, out, wide):
    count, pitch = parts.shape[0], PITCH
    heads = out.shape[1]
    wide[...] = parts[...].astype(jnp.float32).reshape(wide.shape)
    state = wide[pl.ds(heads, count, stride=pitch), :]
    joined = state + pltpu.roll(state, LANES - heads, 1)
    total = pltpu.roll(joined, LANES - 2 * heads, 1)
    place = lax.broadcasted_iota(jnp.int32, (count, LANES), 1)
    m = jnp.where(place < heads, joined, 0.0)
    l = jnp.where(place < heads, total, 1.0)
    factor = jnp.exp2(m - jnp.max(m, axis=0, keepdims=True))
    share = factor / jnp.sum(factor * l, axis=0, keepdims=True)
    turned = share.T[:heads, :]
    y = jnp.zeros((heads, LANES), jnp.float32)
    for k in range(count):
        y += turned[:, k : k + 1] * wide[pl.ds(k * pitch, heads), :]
    out[...] = jnp.broadcast_to(y.astype(jnp.bfloat16)[None], out.shape)


def project(values, w_out, out, wide):
    rows, heads, _ = values.shape
    wide[...] = values[...].astype(jnp.float32).reshape(wide.shape)
    x = jnp.concatenate(
        [wide[pl.ds(h, rows, stride=heads), :].astype(jnp.bfloat16) for h in range(heads)], axis=-1
    )
    y = lax.dot_general(x, w_out[...], NT, preferred_element_type=jnp.float32)
    each = out.shape[1]
    for j in range(out.shape[0]):
        out[j] = y[j * each : (j + 1) * each]


def finish(sums, out):
    y = jnp.sum(sums[...], axis=0).astype(out.dtype)
    for r in range(out.shape[0]):
        out[r] = y[r * out.shape[1] : (r + 1) * out.shape[1]]


def local(
    head_devices,
    latent_cache,
    block_owner,
    block_index,
    cache_lengths,
    query_nope,
    query_rope,
    new_latent,
    w_uk,
    value_up_weight,
    w_out,
):
    steps, requests, heads = query_nope.shape[:3]
    rows = steps * requests
    blocks = latent_cache.shape[0]
    width = KVL + ROPE
    chunks = blocks // min(GROUP, blocks)
    vmem = pl.BlockSpec(memory_space=pltpu.VMEM)
    hbm = pl.BlockSpec(memory_space=pltpu.HBM)
    params = pltpu.CompilerParams(vmem_limit_bytes=VMEM_LIMIT)
    f32, bf16 = jnp.float32, jnp.bfloat16
    message, w_out_near = pl.pallas_call(
        attend,
        out_shape=(
            pltpu.VMEM((rows, PITCH // THIN, THIN, LANES), bf16),
            pltpu.VMEM(w_out.shape[::-1], bf16),
        ),
        in_specs=[hbm] * 10,
        out_specs=(vmem, vmem),
        scratch_shapes=[
            pltpu.SMEM(block_owner.shape, jnp.int32),
            pltpu.SMEM(block_index.shape, jnp.int32),
            pltpu.SMEM(cache_lengths.shape, jnp.int32),
            pltpu.VMEM(query_nope.shape, bf16),
            pltpu.VMEM(query_rope.shape, bf16),
            pltpu.VMEM(new_latent.shape, bf16),
            pltpu.VMEM(w_uk.shape, bf16),
            pltpu.VMEM(value_up_weight.shape, bf16),
            pltpu.VMEM(latent_cache.shape, bf16),
            pltpu.VMEM((rows * heads, LANES), f32),
            pltpu.VMEM((KVL // LANES, rows * heads, LANES), f32),
            pltpu.VMEM((requests, steps * heads, width), bf16),
            pltpu.VMEM((blocks, steps * heads, BLK), f32),
            pltpu.VMEM((requests, steps * heads, BLK), f32),
            pltpu.VMEM((requests, steps * heads, LANES), f32),
            pltpu.VMEM((requests, steps * heads, BLK), f32),
            pltpu.VMEM((KVL // LANES, rows * heads, LANES), f32),
            pltpu.VMEM((rows * PITCH, LANES), f32),
            pltpu.SemaphoreType.DMA((6,)),
            pltpu.SemaphoreType.DMA((KEY_PARTS,)),
            pltpu.SemaphoreType.DMA,
            pltpu.SemaphoreType.DMA,
            pltpu.SemaphoreType.DMA((chunks,)),
        ],
        compiler_params=params,
        name="attend",
    )(
        *(
            pltpu.with_memory_space_constraint(x, pltpu.HBM)
            for x in (
                block_owner,
                block_index,
                cache_lengths,
                query_nope,
                query_rope,
                new_latent,
                w_uk,
                value_up_weight,
                latent_cache,
                w_out.T,
            )
        )
    )
    parts = lax.all_to_all(message, "seq", 0, 0, tiled=True)
    value = pl.pallas_call(
        combine,
        out_shape=jax.ShapeDtypeStruct((rows, heads, VD), bf16),
        in_specs=[vmem],
        out_specs=vmem,
        scratch_shapes=[pltpu.VMEM((rows * PITCH, LANES), f32)],
        compiler_params=pltpu.CompilerParams(vmem_limit_bytes=SMALL_LIMIT),
        name="combine",
    )(parts)
    values = lax.all_to_all(value, "seq", 0, 0, tiled=True)
    sums = pl.pallas_call(
        project,
        out_shape=jax.ShapeDtypeStruct((head_devices, rows // head_devices, w_out.shape[1]), f32),
        in_specs=[vmem, vmem],
        out_specs=vmem,
        scratch_shapes=[pltpu.VMEM((rows * heads, LANES), f32)],
        compiler_params=pltpu.CompilerParams(vmem_limit_bytes=SMALL_LIMIT),
        name="project",
    )(values, w_out_near)
    sums = lax.all_to_all(sums, "head", 0, 0, tiled=True)
    return pl.pallas_call(
        finish,
        out_shape=jax.ShapeDtypeStruct((requests // head_devices, steps, w_out.shape[1]), bf16),
        in_specs=[vmem],
        out_specs=vmem,
        compiler_params=pltpu.CompilerParams(vmem_limit_bytes=SMALL_LIMIT),
        name="finish",
    )(sums)


def solution(mesh):
    in_specs = (
        P("seq", None, None),
        P("seq"),
        P("seq"),
        P(),
        P(None, None, "head", None),
        P(None, None, "head", None),
        P(),
        P("head", None, None),
        P("head", None, None),
        P("head", "seq"),
    )
    out_specs = P("head", None, "seq")
    body = functools.partial(local, mesh.shape["head"])
    return jax.shard_map(body, mesh=mesh, in_specs=in_specs, out_specs=out_specs, check_vma=False)
```

```python
import functools
import math

import jax
import jax.numpy as jnp
from jax import lax
from jax.experimental import pallas as pl
from jax.experimental.pallas import tpu as pltpu
from jax.sharding import PartitionSpec as P

KVL = 512
ROPE = 64
NOPE = 128
VD = 128
BLK = 64
LANES = 128
PITCH = 18
THIN = 2

NEG = -1e30
SCALE = (NOPE + ROPE) ** (-0.5) * math.log2(math.e)
VMEM_LIMIT = 48 * 1024 * 1024
SMALL_LIMIT = 16 * 1024 * 1024
GROUP = 32
KEY_PARTS = 4

NT = (((1,), (1,)), ((), ()))


def attend(
    owner_hbm,
    index_hbm,
    lengths_hbm,
    query_nope_hbm,
    query_rope_hbm,
    new_latent_hbm,
    w_uk_hbm,
    value_up_hbm,
    cache_hbm,
    out,
    owner,
    index,
    lengths,
    query_nope,
    query_rope,
    new_latent,
    w_uk,
    value_up,
    cache,
    nope,
    q_lat,
    q_full,
    scores,
    best,
    top,
    part,
    acc,
    message,
    small_sem,
    key_sem,
    value_sem,
    cache_sem,
):
    blocks = cache.shape[0]
    steps, requests, heads = query_nope_hbm.shape[:3]
    rows = steps * requests
    group = min(GROUP, blocks)
    chunks = blocks // group
    mine = lax.axis_index("seq")

    part_heads = heads // KEY_PARTS

    def copy_small(i, source, target):
        return pltpu.make_async_copy(source, target, small_sem.at[i])

    copy_nope = copy_small(0, query_nope_hbm, query_nope)
    others = [
        copy_small(i + 1, source, target)
        for i, (source, target) in enumerate(
            [
                (owner_hbm, owner),
                (index_hbm, index),
                (lengths_hbm, lengths),
                (query_rope_hbm, query_rope),
                (new_latent_hbm, new_latent),
            ]
        )
    ]

    def copy_uk(i):
        span = pl.ds(i * part_heads, part_heads)
        return pltpu.make_async_copy(w_uk_hbm.at[span], w_uk.at[span], key_sem.at[i])

    copy_up = pltpu.make_async_copy(value_up_hbm, value_up, value_sem)

    def copy_chunk(i):
        span = pl.ds(i * group, group)
        return pltpu.make_async_copy(cache_hbm.at[span], cache.at[span], cache_sem.at[i])

    copy_nope.start()
    for i in range(KEY_PARTS):
        copy_uk(i).start()
    for copy in others:
        copy.start()
    for i in range(chunks):
        copy_chunk(i).start()
    copy_up.start()

    best[...] = jnp.full(best.shape, NEG, jnp.float32)
    part[...] = jnp.zeros(part.shape, jnp.float32)
    acc[...] = jnp.zeros(acc.shape, jnp.float32)
    message[...] = jnp.zeros(message.shape, jnp.float32)

    copy_nope.wait()
    nope[...] = query_nope[...].reshape(rows * heads, NOPE).astype(jnp.float32)
    for h in range(heads):
        if h % part_heads == 0:
            copy_uk(h // part_heads).wait()
        y = jnp.dot(
            nope[pl.ds(h, rows, stride=heads), :].astype(jnp.bfloat16),
            w_uk[h],
            preferred_element_type=jnp.float32,
        )
        for c in range(KVL // LANES):
            q_lat[c, pl.ds(h, rows, stride=heads), :] = y[:, c * LANES : (c + 1) * LANES]
    for copy in others:
        copy.wait()
    for r in range(requests):
        for s in range(steps):
            for c in range(KVL // LANES):
                q_full[r, s * heads : (s + 1) * heads, c * LANES : (c + 1) * LANES] = q_lat[
                    c, (s * requests + r) * heads : (s * requests + r + 1) * heads, :
                ].astype(jnp.bfloat16)
            q_full[r, s * heads : (s + 1) * heads, KVL:] = query_rope[s, r]

    lane = lax.broadcasted_iota(jnp.int32, (steps * heads, BLK), 1)

    def score_chunk(i, carry):
        copy_chunk(i).wait()
        for j in range(group):
            b = i * group + j
            o = owner[b]
            live = lengths[o] - index[b] * BLK
            s = lax.dot_general(q_full[o], cache[b], NT, preferred_element_type=jnp.float32)
            s = jnp.where(lane < live, s * SCALE, NEG)
            scores[b] = s
            best[o] = jnp.maximum(best[o], s)
        return carry

    for i in range(chunks):
        score_chunk(i, 0)

    taken = jnp.minimum(mine, requests - 1)
    shape = (steps * heads, steps * requests)
    token = lax.broadcasted_iota(jnp.int32, shape, 1)
    step = lax.broadcasted_iota(jnp.int32, shape, 0) // heads
    allowed = (token % requests == mine) & (token // requests <= step)
    keys = new_latent[...].reshape(steps * requests, KVL + ROPE)
    fresh = lax.dot_general(q_full[taken], keys, NT, preferred_element_type=jnp.float32)
    fresh = jnp.where(allowed, fresh * SCALE, NEG)
    best[taken, :, : steps * requests] = jnp.maximum(best[taken, :, : steps * requests], fresh)

    m = jnp.max(best[...], axis=-1, keepdims=True)
    high = m.astype(jnp.bfloat16).astype(jnp.float32)
    low = (m - high).astype(jnp.bfloat16).astype(jnp.float32)
    top[...] = jnp.broadcast_to(high + low, top.shape)

    def add(o, weights, values):
        y = jnp.dot(weights.astype(jnp.bfloat16), values, preferred_element_type=jnp.float32)
        span = pl.ds(pl.multiple_of(o * (steps * heads), steps * heads), steps * heads)
        for c in range(KVL // LANES):
            acc[c, span, :] += y[:, c * LANES : (c + 1) * LANES]

    def add_chunk(i, carry):
        for j in range(min(64, blocks)):
            b = i * min(64, blocks) + j
            o = owner[b]
            weights = jnp.exp2(scores[b] - top[o, :, :BLK])
            part[o] += weights
            add(o, weights, cache[b, :, :KVL])
        return carry

    lax.fori_loop(0, blocks // min(64, blocks), add_chunk, 0)
    weights = jnp.where(allowed, jnp.exp2(fresh - top[taken, :, : steps * requests]), 0.0)
    part[taken, :, : steps * requests] += weights
    add(taken, weights, keys[:, :KVL])

    total = jnp.sum(part[...], axis=-1, keepdims=True)
    best_rows = jnp.broadcast_to(total, top.shape).reshape(rows * heads, LANES)
    nope[...] = best_rows
    q_lat[0] = top[...].reshape(rows * heads, LANES)
    place = lax.broadcasted_iota(jnp.int32, (rows, LANES), 1)
    m_of = jnp.zeros((rows, LANES), jnp.float32)
    l_of = jnp.zeros((rows, LANES), jnp.float32)
    copy_up.wait()
    for h in range(heads):
        every = pl.ds(h, rows, stride=heads)
        x = jnp.concatenate([acc[c, every, :].astype(jnp.bfloat16) for c in range(KVL // LANES)], axis=-1)
        y = jnp.dot(x, value_up[h], preferred_element_type=jnp.float32)
        message[pl.ds(h, rows, stride=PITCH), :] = y
        m_of = jnp.where(place % heads == h, q_lat[0, every, :], m_of)
        l_of = jnp.where(place % heads == h, nope[every, :], l_of)
    m_high = m_of.astype(jnp.bfloat16).astype(jnp.float32)
    l_high = l_of.astype(jnp.bfloat16).astype(jnp.float32)
    kind = place // heads
    state = jnp.where(kind == 0, m_high, jnp.where(kind == 1, m_of - m_high, jnp.where(kind == 2, l_high, l_of - l_high)))
    message[pl.ds(heads, rows, stride=PITCH), :] = state
    out[...] = message[...].reshape(out.shape).astype(jnp.bfloat16)


def combine(parts, out, wide):
    count, pitch = parts.shape[0], PITCH
    heads = out.shape[1]
    wide[...] = parts[...].astype(jnp.float32).reshape(wide.shape)
    state = wide[pl.ds(heads, count, stride=pitch), :]
    joined = state + pltpu.roll(state, LANES - heads, 1)
    total = pltpu.roll(joined, LANES - 2 * heads, 1)
    place = lax.broadcasted_iota(jnp.int32, (count, LANES), 1)
    m = jnp.where(place < heads, joined, 0.0)
    l = jnp.where(place < heads, total, 1.0)
    factor = jnp.exp2(m - jnp.max(m, axis=0, keepdims=True))
    share = factor / jnp.sum(factor * l, axis=0, keepdims=True)
    turned = share.T[:heads, :]
    y = jnp.zeros((heads, LANES), jnp.float32)
    for k in range(count):
        y += turned[:, k : k + 1] * wide[pl.ds(k * pitch, heads), :]
    out[...] = jnp.broadcast_to(y.astype(jnp.bfloat16)[None], out.shape)


def project(values, w_out, out, wide):
    rows, heads, _ = values.shape
    wide[...] = values[...].astype(jnp.float32).reshape(wide.shape)
    x = jnp.concatenate(
        [wide[pl.ds(h, rows, stride=heads), :].astype(jnp.bfloat16) for h in range(heads)], axis=-1
    )
    y = lax.dot_general(x, w_out[...], NT, preferred_element_type=jnp.float32)
    each = out.shape[1]
    for j in range(out.shape[0]):
        out[j] = y[j * each : (j + 1) * each].astype(out.dtype)


def finish(sums, out):
    y = jnp.sum(sums[...].astype(jnp.float32), axis=0).astype(out.dtype)
    for r in range(out.shape[0]):
        out[r] = y[r * out.shape[1] : (r + 1) * out.shape[1]]


def local(
    head_devices,
    latent_cache,
    block_owner,
    block_index,
    cache_lengths,
    query_nope,
    query_rope,
    new_latent,
    w_uk,
    value_up_weight,
    w_out,
):
    steps, requests, heads = query_nope.shape[:3]
    rows = steps * requests
    blocks = latent_cache.shape[0]
    width = KVL + ROPE
    chunks = blocks // min(GROUP, blocks)
    vmem = pl.BlockSpec(memory_space=pltpu.VMEM)
    hbm = pl.BlockSpec(memory_space=pltpu.HBM)
    params = pltpu.CompilerParams(vmem_limit_bytes=VMEM_LIMIT)
    f32, bf16 = jnp.float32, jnp.bfloat16
    message = pl.pallas_call(
        attend,
        out_shape=pltpu.VMEM((rows, PITCH // THIN, THIN, LANES), bf16),
        in_specs=[hbm] * 9,
        out_specs=vmem,
        scratch_shapes=[
            pltpu.SMEM(block_owner.shape, jnp.int32),
            pltpu.SMEM(block_index.shape, jnp.int32),
            pltpu.SMEM(cache_lengths.shape, jnp.int32),
            pltpu.VMEM(query_nope.shape, bf16),
            pltpu.VMEM(query_rope.shape, bf16),
            pltpu.VMEM(new_latent.shape, bf16),
            pltpu.VMEM(w_uk.shape, bf16),
            pltpu.VMEM(value_up_weight.shape, bf16),
            pltpu.VMEM(latent_cache.shape, bf16),
            pltpu.VMEM((rows * heads, LANES), f32),
            pltpu.VMEM((KVL // LANES, rows * heads, LANES), f32),
            pltpu.VMEM((requests, steps * heads, width), bf16),
            pltpu.VMEM((blocks, steps * heads, BLK), f32),
            pltpu.VMEM((requests, steps * heads, BLK), f32),
            pltpu.VMEM((requests, steps * heads, LANES), f32),
            pltpu.VMEM((requests, steps * heads, BLK), f32),
            pltpu.VMEM((KVL // LANES, rows * heads, LANES), f32),
            pltpu.VMEM((rows * PITCH, LANES), f32),
            pltpu.SemaphoreType.DMA((6,)),
            pltpu.SemaphoreType.DMA((KEY_PARTS,)),
            pltpu.SemaphoreType.DMA,
            pltpu.SemaphoreType.DMA((chunks,)),
        ],
        compiler_params=params,
        name="attend",
    )(
        *(
            pltpu.with_memory_space_constraint(x, pltpu.HBM)
            for x in (
                block_owner,
                block_index,
                cache_lengths,
                query_nope,
                query_rope,
                new_latent,
                w_uk,
                value_up_weight,
                latent_cache,
            )
        )
    )
    parts = lax.all_to_all(message, "seq", 0, 0, tiled=True)
    value = pl.pallas_call(
        combine,
        out_shape=jax.ShapeDtypeStruct((rows, heads, VD), bf16),
        in_specs=[vmem],
        out_specs=vmem,
        scratch_shapes=[pltpu.VMEM((rows * PITCH, LANES), f32)],
        compiler_params=pltpu.CompilerParams(vmem_limit_bytes=SMALL_LIMIT),
        name="combine",
    )(parts)
    values = lax.all_to_all(value, "seq", 0, 0, tiled=True)
    sums = pl.pallas_call(
        project,
        out_shape=jax.ShapeDtypeStruct((head_devices, rows // head_devices, w_out.shape[1]), bf16),
        in_specs=[vmem, vmem],
        out_specs=vmem,
        scratch_shapes=[pltpu.VMEM((rows * heads, LANES), f32)],
        compiler_params=pltpu.CompilerParams(vmem_limit_bytes=SMALL_LIMIT),
        name="project",
    )(values, w_out.T)
    sums = lax.all_to_all(sums, "head", 0, 0, tiled=True)
    return pl.pallas_call(
        finish,
        out_shape=jax.ShapeDtypeStruct((requests // head_devices, steps, w_out.shape[1]), bf16),
        in_specs=[vmem],
        out_specs=vmem,
        compiler_params=pltpu.CompilerParams(vmem_limit_bytes=SMALL_LIMIT),
        name="finish",
    )(sums)


def solution(mesh):
    in_specs = (
        P("seq", None, None),
        P("seq"),
        P("seq"),
        P(),
        P(None, None, "head", None),
        P(None, None, "head", None),
        P(),
        P("head", None, None),
        P("head", None, None),
        P("head", "seq"),
    )
    out_specs = P("head", None, "seq")
    body = functools.partial(local, mesh.shape["head"])
    return jax.shard_map(body, mesh=mesh, in_specs=in_specs, out_specs=out_specs, check_vma=False)
```
